256 devices in a mesh: row: 4 (over x), col: 2 (over core), depth: 32 (over z, y).
Axes of the slice: x: 4, y: 4, z: 8, core: 2. Of those that a mesh axis runs over, the one named last changes fastest.
Arguments:
- residual_in: float32 [32768, 6400], P(('col', 'depth'), 'row'), may hold values from -6 to 6
- integrals: bfloat16 [6400, 6400], P('row', ('col', 'depth')), may hold values from -0.078125 to 0.078125
- amplitudes: bfloat16 [6400, 32768], P('row', ('col', 'depth')), may hold values from -16 to 16
Outputs:
- residual_out: float32 [32768, 6400], P(('col', 'depth'), 'row')
The draws below stay inside these ranges and needn't reach their ends.
All inputs are finite; a program needn't handle non-finite values.
Results may differ from the reference program's by a relative error of at most 0.0003.
Values may be sent and summed in bfloat16 or wider, within the bound.
No kernel may reach another device: no remote copies, remote signals or barrier semaphores. Data moves between devices by JAX's collectives and lax.ppermute only.
A program may use at most 128 MiB of HBM per device.

```python
import jax
import jax.numpy as jnp
from jax import lax

M = 6400
K = 6400
NPAIRS = 32768


def strengthened(result, key, source, target, blocks, factor):
    owner, partner = [(jnp.arange(result.shape[position]) // (result.shape[position] // blocks)).reshape([-1 if axis == position else 1 for axis in range(result.ndim)]) for position in (source, target)]
    chosen = jax.random.permutation(key, blocks)[partner]
    strong = (owner == chosen) | (owner == (partner + blocks // 2) % blocks)
    return jnp.where(strong, factor * result, result)


def block_levels(rng, shape, shards, smallest, largest):
    factor_of, own = 1.0, jax.random.fold_in(rng, 6)
    for position, shards_of in shards:
        steps = jnp.exp(jax.random.uniform(jax.random.fold_in(own, position), (shards_of,), jnp.float32, smallest / len(shards), largest / len(shards)))
        factor_of = factor_of * jnp.repeat(steps, shape[position] // shards_of).reshape([-1 if axis == position else 1 for axis in range(len(shape))])
    return factor_of


def centred(stream_key, shape, deviation, bound, shards=(), held_as=jnp.bfloat16):
    result = deviation * jax.random.normal(stream_key, shape, jnp.float32)
    if shards:
        result = result * block_levels(stream_key, shape, shards, -0.22, 0.18)
    return jnp.clip(result, -bound, bound).astype(held_as)


def noise_with(key, dims, deviation, most, pieces, heavy, dtype=jnp.bfloat16):
    array = deviation * jax.random.normal(key, dims, jnp.float32)
    if pieces:
        array = array * block_levels(key, dims, pieces, -0.22, 0.18)
    return jnp.clip(strengthened(array, jax.random.fold_in(key, 3), *heavy), -most, most).astype(dtype)


def setup_inputs(seed: int = 0) -> dict:
    splits = jax.random.split(jax.random.key(seed), 4)
    residual_in = centred(splits[0], (NPAIRS, M), 1.0, 6.0, ((0, 64), (1, 4)), jnp.float32)
    integrals = centred(splits[1], (M, K), K ** -0.5, 0.078125, ((0, 4), (1, 64)))
    amplitudes = noise_with(splits[2], (K, NPAIRS), 1.0, 16.0, ((0, 4), (1, 64)), (0, 1, 64, 4.0))
    return {"residual_in": residual_in, "integrals": integrals, "amplitudes": amplitudes}


def reference(residual_in, integrals, amplitudes):
    ladder = lax.dot_general(amplitudes, integrals, (((0,), (1,)), ((), ())), preferred_element_type=jnp.float32)
    return residual_in + ladder
```

```python
import jax
import jax.numpy as jnp
from jax import lax
from jax.sharding import PartitionSpec as P


def shift(array, axis, size, step):
    return lax.ppermute(array, axis, [(i, (i + step) % size) for i in range(size)])


def padded(blocks, rows):
    extra = -rows % 8
    parts = blocks.reshape(-1, rows, blocks.shape[-1])
    return jnp.pad(parts, ((0, 0), (0, extra), (0, 0))).reshape(-1, blocks.shape[-1])


def row_panel(block, size):
    after, before = shift(block, "row", size, -1), shift(block, "row", size, 1)
    half = block.shape[0] // 2
    far = [shift(before[:half], "row", size, 1), shift(after[half:], "row", size, -1)]
    ring = jnp.concatenate([block, after, *far, before])
    start = (size - lax.axis_index("row")) % size * block.shape[0]
    return lax.dynamic_slice_in_dim(jnp.concatenate([ring, ring]), start, ring.shape[0])


def solution(mesh):
    size = mesh.shape["row"]

    def per_device(residual_in, integrals, amplitudes):
        rows = integrals.shape[1]
        columns = padded(integrals.T, rows)
        gathered = lax.all_gather(columns, ("col", "depth"), axis=0, tiled=True)
        panel = row_panel(padded(amplitudes, rows), size)
        share = lax.dot_general(
            panel, gathered, (((0,), (0,)), ((), ())), preferred_element_type=jnp.float32
        )
        return residual_in + share

    placed = (P(("col", "depth"), "row"), P("row", ("col", "depth")), P("row", ("col", "depth")))
    return jax.shard_map(
        per_device, mesh=mesh, in_specs=placed, out_specs=P(("col", "depth"), "row"), check_vma=False
    )
```

```python
import jax
import jax.numpy as jnp
from jax import lax
from jax.experimental import pallas as pl
from jax.experimental.pallas import tpu as pltpu
from jax.sharding import PartitionSpec as P

Z, Y = 8, 4


def shift(array, size, step):
    return lax.ppermute(array, "row", [(i, (i + step) % size) for i in range(size)])


def travel(array, first, second):
    pairs = []
    for core, step in enumerate((first, second)):
        if step is not None:
            for z in range(Z):
                for y in range(Y):
                    target = (z + step[0]) % Z * Y + (y + step[1]) % Y
                    pairs.append(((core * Z + z) * Y + y, core * Z * Y + target))
    return lax.ppermute(array, ("col", "depth"), pairs)


def swap(array):
    return lax.ppermute(array, "col", [(0, 1), (1, 0)])


def padded(blocks, rows):
    parts = blocks.reshape(-1, rows, blocks.shape[-1])
    return jnp.pad(parts, ((0, 0), (0, -rows % 8), (0, 0)))


def pieces_of(block):
    along, back = ((0, 1), (1, 0)), ((0, -1), (-1, 0))
    a1 = travel(block, *along)
    b1 = travel(block, *back)
    a2 = travel(a1, *along)
    pack = jnp.concatenate([block, a1, b1, a2])
    b2 = travel(b1, None, back[1])
    a3 = travel(a2, None, along[1])
    b3 = travel(b2, None, back[1])
    a4 = travel(a3, None, along[1])
    rest = jnp.concatenate([b2, a3, b3, a4])
    up, down = ((1, 0), (0, 1)), ((-1, 0), (0, -1))
    u1, d1 = travel(pack, *up), travel(pack, *down)
    u2, d2 = travel(u1, *up), travel(d1, down[0], None)
    first = lax.axis_index("col") == 0
    kept = jnp.where(first, d2, rest)
    u3, d3 = travel(jnp.where(first, u2, rest), *up), travel(kept, *down)
    u4, d4 = travel(u3[:2], *up), travel(d3[2:], *down)
    return [pack, u1, d1, u2, kept, u3, d3, u4, d4]


def arrange(own, after, far_low, far_high, before, rows):
    count, height, width = own.shape

    def kernel(own_ref, after_ref, low_ref, high_ref, before_ref, out_ref, sems):
        x, core, depth = (lax.axis_index(name) for name in ("row", "col", "depth"))
        z, y = depth // Y, depth % Y
        copies = []
        sources = [(own_ref, 0, 0), (after_ref, 1, 0), (low_ref, 2, 0), (high_ref, 2, count // 2), (before_ref, 3, 0)]
        for ref, step, start in sources:
            block_row = lax.rem(x + step, rows)
            half = block_row // (rows // 2)
            for i in range(ref.shape[0]):
                there = lax.rem(block_row, rows // 2) * count + start + i
                dz = lax.rem(there // Y - z + Z, Z)
                dy = lax.rem((start + i) % Y - y + Y, Y)
                oz = jnp.where(dz < Z // 2, 2 * dz, 2 * (Z - dz) - 1)
                oy = jnp.where(dy < Y // 2, 2 * dy, 2 * (Y - dy) - 1)
                place = jnp.where(half == 0, oz * Y + oy, oz // Y * (Y * Y) + oy * Y + lax.rem(oz, Y))
                copy = pltpu.make_async_copy(
                    ref.at[i], out_ref.at[lax.rem(half + core, 2), place], sems.at[len(copies)]
                )
                copy.start()
                copies.append(copy)
        for copy in copies:
            copy.wait()

    return pl.pallas_call(
        kernel,
        out_shape=jax.ShapeDtypeStruct((2, Z * Y, height, width), own.dtype),
        in_specs=[pl.BlockSpec(memory_space=pl.ANY)] * 5,
        out_specs=pl.BlockSpec(memory_space=pl.ANY),
        scratch_shapes=[pltpu.SemaphoreType.DMA((rows * count,))],
        cost_estimate=pl.CostEstimate(flops=0, bytes_accessed=4 * rows * own.size, transcendentals=0),
        name="arrange",
    )(own, after, far_low, far_high, before)


def accumulate(total, factors, pieces, tile=256):
    columns, pairs = total.shape
    pieces = [piece.reshape(-1, columns) for piece in pieces]
    heights = [piece.shape[0] for piece in pieces]

    def kernel(total_ref, *refs):
        piece_refs, factor_refs, out_ref = refs[: len(pieces)], refs[len(pieces) : -1], refs[-1]
        result = total_ref[...]
        at = [0] * len(factors)
        for number, (ref, height) in enumerate(zip(piece_refs, heights)):
            which = number * len(factors) // len(pieces)
            factor = factor_refs[which][pl.ds(at[which], height), :]
            at[which] += height
            result += lax.dot_general(ref[...], factor, (((0,), (0,)), ((), ())), preferred_element_type=jnp.float32)
        out_ref[...] = result

    flops = 2 * columns * pairs * sum(heights)
    return pl.pallas_call(
        kernel,
        grid=(pl.cdiv(columns, tile),),
        out_shape=jax.ShapeDtypeStruct(total.shape, total.dtype),
        in_specs=[pl.BlockSpec((tile, pairs), lambda i: (i, 0))]
        + [pl.BlockSpec((height, tile), lambda i: (0, i)) for height in heights]
        + [pl.BlockSpec(factor.shape, lambda i: (0, 0)) for factor in factors],
        out_specs=pl.BlockSpec((tile, pairs), lambda i: (i, 0)),
        compiler_params=pltpu.CompilerParams(vmem_limit_bytes=48 << 20),
        cost_estimate=pl.CostEstimate(
            flops=flops, bytes_accessed=8 * total.size + 2 * sum(heights) * (columns + pairs), transcendentals=0
        ),
        name="accumulate",
    )(total, *pieces, *factors)


def solution(mesh):
    rows = mesh.shape["row"]

    def per_device(residual_in, integrals, amplitudes):
        depth = integrals.shape[1]
        own = padded(amplitudes, depth)
        after, before = shift(own, rows, -1), shift(own, rows, 1)
        half = own.shape[0] // 2
        far_low, far_high = shift(before[:half], rows, 1), shift(after[half:], rows, -1)
        mine = pieces_of(padded(integrals.T, depth))
        other = [swap(piece) for piece in mine]
        panel = arrange(own, after, far_low, far_high, before, rows)
        panel = panel.reshape(2, -1, panel.shape[-1])
        early = 5
        split = sum(piece.shape[0] for piece in mine[:early]) * own.shape[1]
        total = accumulate(residual_in.T, [panel[0, :split], panel[1, :split]], mine[:early] + other[:early])
        total = accumulate(total, [panel[0, split:], panel[1, split:]], mine[early:] + other[early:])
        return total.T

    placed = (P(("col", "depth"), "row"), P("row", ("col", "depth")), P("row", ("col", "depth")))
    return jax.shard_map(
        per_device, mesh=mesh, in_specs=placed, out_specs=P(("col", "depth"), "row"), check_vma=False
    )
```

```python
import jax
import jax.numpy as jnp
from jax import lax
from jax.experimental import pallas as pl
from jax.experimental.pallas import tpu as pltpu
from jax.sharding import PartitionSpec as P

Z, Y = 8, 4
VMEM = 16 << 20


def shift(array, size, step):
    return lax.ppermute(array, "row", [(i, (i + step) % size) for i in range(size)])


def travel(array, first, second):
    pairs = []
    for core, step in enumerate((first, second)):
        if step is not None:
            for z in range(Z):
                for y in range(Y):
                    target = (z + step[0]) % Z * Y + (y + step[1]) % Y
                    pairs.append(((core * Z + z) * Y + y, core * Z * Y + target))
    return lax.ppermute(array, ("col", "depth"), pairs)


def swap(array):
    return lax.ppermute(array, "col", [(0, 1), (1, 0)])


def padded(blocks, rows):
    parts = blocks.reshape(-1, rows, blocks.shape[-1])
    return jnp.pad(parts, ((0, 0), (0, -rows % 8), (0, 0)))


def gather(block, amplitudes, rows):
    along, back = ((0, 1), (1, 0)), ((0, -1), (-1, 0))
    after, before = shift(amplitudes, rows, -1), shift(amplitudes, rows, 1)
    a1 = travel(block, *along)
    b1 = travel(block, *back)
    a2 = travel(a1, *along)
    pack = jnp.concatenate([block, a1, b1, a2])
    b2 = travel(b1, None, back[1])
    a3 = travel(a2, None, along[1])
    b3 = travel(b2, None, back[1])
    a4 = travel(a3, None, along[1])
    rest = jnp.concatenate([b2, a3, b3, a4])
    up, down = ((1, 0), (0, 1)), ((-1, 0), (0, -1))
    u1, d1 = travel(pack, *up), travel(pack, *down)
    u2, d2 = travel(u1, *up), travel(d1, down[0], None)
    u2, d2, after, before = lax.optimization_barrier((u2, d2, after, before))
    half = amplitudes.shape[0] // 2
    far_low, far_high = shift(before[:half], rows, 1), shift(after[half:], rows, -1)
    first = lax.axis_index("col") == 0
    kept = jnp.where(first, d2, rest)
    u3, d3 = travel(jnp.where(first, u2, rest), *up), travel(kept, *down)
    u3, d3, far_low, far_high = lax.optimization_barrier((u3, d3, far_low, far_high))
    u4, d4 = travel(u3[:2], *up), travel(d3[2:], *down)
    return [pack, u1, d1, u2, kept, u3, d3, u4, d4], (after, far_low, far_high, before)


def arrange(own, after, far_low, far_high, before, rows, height, cuts):
    width = own.shape[1]
    count = own.shape[0] // height
    full = height + -height % 8

    def kernel(own_ref, after_ref, low_ref, high_ref, before_ref, *refs):
        out_refs, held = refs[:-1], refs[-1]
        x, core, depth = (lax.axis_index(name) for name in ("row", "col", "depth"))
        z, y = depth // Y, lax.rem(depth, Y)
        held[:, :, height:, :] = jnp.zeros((2, Z * Y, full - height, width), held.dtype)
        sources = [(own_ref, 0, 0), (after_ref, 1, 0), (low_ref, 2, 0), (high_ref, 2, count // 2), (before_ref, 3, 0)]
        for ref, step, start in sources:
            block_row = lax.rem(x + step, rows)
            half = block_row // (rows // 2)
            for i in range(ref.shape[0] // height):
                there = lax.rem(block_row, rows // 2) * count + start + i
                dz = lax.rem(there // Y - z + Z, Z)
                dy = lax.rem((start + i) % Y - y + Y, Y)
                oz = jnp.where(dz < Z // 2, 2 * dz, 2 * (Z - dz) - 1)
                oy = jnp.where(dy < Y // 2, 2 * dy, 2 * (Y - dy) - 1)
                place = jnp.where(half == 0, oz * Y + oy, oz // Y * (Y * Y) + oy * Y + lax.rem(oz, Y))
                held[lax.rem(half + core, 2), place, pl.ds(0, height), :] = ref[pl.ds(i * height, height), :]
        for side in range(2):
            at = 0
            for out_ref, blocks in zip(out_refs, cuts):
                part = held[side, pl.ds(at, blocks)].reshape(blocks * full, width)
                out_ref[side] = part.T
                at += blocks

    size = 2 * own.size * rows
    return pl.pallas_call(
        kernel,
        out_shape=[jax.ShapeDtypeStruct((2, width, blocks * full), own.dtype) for blocks in cuts],
        scratch_shapes=[pltpu.VMEM((2, Z * Y, full, width), own.dtype)],
        compiler_params=pltpu.CompilerParams(vmem_limit_bytes=VMEM),
        cost_estimate=pl.CostEstimate(flops=0, bytes_accessed=2 * size, transcendentals=0),
        name="arrange",
    )(own, after, far_low, far_high, before)


def accumulate(total, factor, mine, other, tile=256):
    columns, pairs = total.shape
    pieces = [piece.reshape(-1, columns) for piece in mine + other]
    depth = factor.shape[-1]

    def kernel(total_ref, factor_ref, *refs):
        piece_refs, out_ref = refs[:-1], refs[-1]

        def add(start, width):
            share = jnp.zeros((pairs, width), jnp.float32)
            for side in range(2):
                refs = piece_refs[side * len(mine) :][: len(mine)]
                part = jnp.concatenate([ref[:, pl.ds(start, width)] for ref in refs])
                share += jnp.dot(factor_ref[side], part, preferred_element_type=jnp.float32)
            out_ref[pl.ds(start, width), :] = total_ref[pl.ds(start, width), :] + share.T

        whole = columns // tile

        @pl.loop(0, whole)
        def _(i):
            add(pl.multiple_of(i * tile, tile), tile)

        if columns % tile:
            add(whole * tile, columns % tile)

    return pl.pallas_call(
        kernel,
        out_shape=jax.ShapeDtypeStruct(total.shape, total.dtype),
        compiler_params=pltpu.CompilerParams(vmem_limit_bytes=VMEM),
        cost_estimate=pl.CostEstimate(
            flops=4 * columns * pairs * depth,
            bytes_accessed=8 * total.size + 4 * depth * (columns + pairs),
            transcendentals=0,
        ),
        name="accumulate",
    )(total, factor, *pieces)


def solution(mesh):
    rows = mesh.shape["row"]

    def per_device(residual_in, integrals, amplitudes):
        height = integrals.shape[1]
        mine, others = gather(padded(integrals.T, height), amplitudes, rows)
        other = [swap(piece) for piece in mine]
        factors = arrange(amplitudes, *others, rows, height, [20, 8, 4])
        total = residual_in.T
        for factor, a, b in zip(factors, (0, 5, 7), (5, 7, 9)):
            total = accumulate(total, factor, mine[a:b], other[a:b])
        return total.T

    placed = (P(("col", "depth"), "row"), P("row", ("col", "depth")), P("row", ("col", "depth")))
    return jax.shard_map(
        per_device, mesh=mesh, in_specs=placed, out_specs=P(("col", "depth"), "row"), check_vma=False
    )
```

```python
import jax
import jax.numpy as jnp
from jax import lax
from jax.experimental import pallas as pl
from jax.experimental.pallas import tpu as pltpu
from jax.sharding import PartitionSpec as P

Z, Y = 8, 4
VMEM = 16 << 20
LONGER = 192


def shift(array, size, step):
    return lax.ppermute(array, "row", [(i, (i + step) % size) for i in range(size)])


def travel(array, first, second):
    pairs = []
    for core, step in enumerate((first, second)):
        if step is not None:
            for z in range(Z):
                for y in range(Y):
                    target = (z + step[0]) % Z * Y + (y + step[1]) % Y
                    pairs.append(((core * Z + z) * Y + y, core * Z * Y + target))
    return lax.ppermute(array, ("col", "depth"), pairs)


def swap(array):
    return lax.ppermute(array, "col", [(0, 1), (1, 0)])


def padded(blocks, rows):
    parts = blocks.reshape(-1, rows, blocks.shape[-1])
    return jnp.pad(parts, ((0, 0), (0, -rows % 8), (0, 0)))


def gather(block, height, amplitudes, rows, multiply_first):
    count = amplitudes.shape[0]
    along, back = ((0, 1), (1, 0)), ((0, -1), (-1, 0))
    up, down = ((1, 0), (0, 1)), ((-1, 0), (0, -1))
    longer = jnp.pad(amplitudes, ((0, LONGER), (0, 0)))
    after, before = shift(longer, rows, -1), shift(longer, rows, 1)
    a1 = travel(block, *along)
    b1 = travel(block, *back)
    a2 = travel(a1, *along)
    pack = jnp.concatenate([block, a1, b1, a2])
    b2 = travel(b1, None, back[1])
    a3 = travel(a2, None, along[1])
    b3 = travel(b2, None, back[1])
    a4 = travel(a3, None, along[1])
    rest = jnp.concatenate([b2, a3, b3, a4])
    u1, d1 = travel(pack, *up), travel(pack, *down)
    u2, d2 = travel(u1, *up), travel(d1, down[0], None)
    far_low, far_high = shift(before[: count // 2], rows, 1), shift(after[count // 2 : count], rows, -1)
    u2, d2, far_low, far_high = lax.optimization_barrier((u2, d2, far_low, far_high))
    first = lax.axis_index("col") == 0
    kept = jnp.where(first, d2, rest)
    u3, d3 = travel(jnp.where(first, u2, rest), *up), travel(kept, *down)
    factors = arrange(amplitudes, after, far_low, far_high, before, rows, height, [20, 8, 4])
    early = [pack, u1, d1, u2, kept]
    total = multiply_first(factors[0], early + [swap(piece) for piece in early])
    u3, d3, total = lax.optimization_barrier((u3, d3, total))
    u4, d4 = travel(u3[:2], *up), travel(d3[2:], *down)
    return factors[1:], total, [u3, d3, swap(u3), swap(d3)], [u4, d4, swap(u4), swap(d4)]


def arrange(own, after, far_low, far_high, before, rows, height, cuts):
    width = own.shape[1]
    count = own.shape[0] // height
    full = height + -height % 8

    def kernel(own_ref, after_ref, low_ref, high_ref, before_ref, *refs):
        out_refs, held = refs[:-1], refs[-1]
        x, core, depth = (lax.axis_index(name) for name in ("row", "col", "depth"))
        z, y = depth // Y, lax.rem(depth, Y)
        held[:, :, height:, :] = jnp.zeros((2, Z * Y, full - height, width), held.dtype)
        sources = [(own_ref, 0, 0), (after_ref, 1, 0), (low_ref, 2, 0), (high_ref, 2, count // 2), (before_ref, 3, 0)]
        for ref, step, start in sources:
            block_row = lax.rem(x + step, rows)
            half = block_row // (rows // 2)
            for i in range(min(count, ref.shape[0] // height)):
                there = lax.rem(block_row, rows // 2) * count + start + i
                dz = lax.rem(there // Y - z + Z, Z)
                dy = lax.rem((start + i) % Y - y + Y, Y)
                oz = jnp.where(dz < Z // 2, 2 * dz, 2 * (Z - dz) - 1)
                oy = jnp.where(dy < Y // 2, 2 * dy, 2 * (Y - dy) - 1)
                place = jnp.where(half == 0, oz * Y + oy, oz // Y * (Y * Y) + oy * Y + lax.rem(oz, Y))
                held[lax.rem(half + core, 2), place, pl.ds(0, height), :] = ref[pl.ds(i * height, height), :]
        for side in range(2):
            at = 0
            for out_ref, blocks in zip(out_refs, cuts):
                part = held[side, pl.ds(at, blocks)].reshape(blocks * full, width)
                out_ref[side] = part.T
                at += blocks

    size = 2 * own.size * rows
    return pl.pallas_call(
        kernel,
        out_shape=[jax.ShapeDtypeStruct((2, width, blocks * full), own.dtype) for blocks in cuts],
        scratch_shapes=[pltpu.VMEM((2, Z * Y, full, width), own.dtype)],
        compiler_params=pltpu.CompilerParams(vmem_limit_bytes=VMEM),
        cost_estimate=pl.CostEstimate(flops=0, bytes_accessed=2 * size, transcendentals=0),
        name="arrange",
    )(own, after, far_low, far_high, before)


def products(factor_ref, piece_refs, start, width):
    share = 0.0
    count = len(piece_refs) // 2
    for side in range(2):
        part = jnp.concatenate([ref[:, pl.ds(start, width)] for ref in piece_refs[side * count :][:count]])
        share += jnp.dot(factor_ref[side], part, preferred_element_type=jnp.float32)
    return share


def multiply(body, shape, factor, pieces, *operands, **options):
    columns = pieces[0].shape[-1]
    flops = 4 * factor.shape[1] * factor.shape[2] * columns
    return pl.pallas_call(
        body,
        out_shape=jax.ShapeDtypeStruct(shape, jnp.float32),
        compiler_params=pltpu.CompilerParams(vmem_limit_bytes=VMEM),
        cost_estimate=pl.CostEstimate(flops=flops, bytes_accessed=flops // 512, transcendentals=0),
        **options,
    )(*operands, factor, *[piece.reshape(-1, columns) for piece in pieces])


def tiles(columns, tile=256):
    return [(start, min(tile, columns - start)) for start in range(0, columns, tile)]


def first_products(factor, pieces):
    def body(factor_ref, *refs):
        for start, width in tiles(refs[-1].shape[1]):
            refs[-1][:, pl.ds(start, width)] = products(factor_ref, refs[:-1], start, width)

    return multiply(body, (factor.shape[1], pieces[0].shape[-1]), factor, pieces, name="first")


def more_products(residual, total, factor, pieces):
    def body(residual_ref, total_ref, factor_ref, *refs):
        for start, width in tiles(refs[-1].shape[0]):
            part = pl.ds(start, width)
            share = total_ref[:, part] + products(factor_ref, refs[:-1], start, width)
            refs[-1][part, :] = residual_ref[part, :] + share.T

    return multiply(body, residual.shape, factor, pieces, residual, total, name="more")


def last_products(total, factor, pieces):
    parts = tiles(total.shape[0])

    def body(total_ref, factor_ref, *refs):
        *piece_refs, out_ref, held, sems = refs
        copies = []
        for number, (start, width) in enumerate(parts):
            part = pl.ds(start, width)
            held[part, :] = total_ref[part, :] + products(factor_ref, piece_refs, start, width).T
            copies.append(pltpu.make_async_copy(held.at[part], out_ref.at[part], sems.at[number]))
            copies[-1].start()
        for copy in copies:
            copy.wait()

    return multiply(
        body,
        total.shape,
        factor,
        pieces,
        total,
        out_specs=pl.BlockSpec(memory_space=pl.ANY),
        scratch_shapes=[pltpu.VMEM(total.shape, jnp.float32), pltpu.SemaphoreType.DMA((len(parts),))],
        name="last",
    )


def solution(mesh):
    rows = mesh.shape["row"]

    def per_device(residual_in, integrals, amplitudes):
        height = integrals.shape[1]
        block = padded(integrals.T, height)
        factors, total, more, last = gather(block, height, amplitudes, rows, first_products)
        total = more_products(residual_in.T, total, factors[0], more)
        return last_products(total, factors[1], last).T

    placed = (P(("col", "depth"), "row"), P("row", ("col", "depth")), P("row", ("col", "depth")))
    return jax.shard_map(
        per_device, mesh=mesh, in_specs=placed, out_specs=P(("col", "depth"), "row"), check_vma=False
    )
```

```python
import jax
import jax.numpy as jnp
from jax import lax
from jax.experimental import pallas as pl
from jax.experimental.pallas import tpu as pltpu
from jax.sharding import PartitionSpec as P

Z, Y = 8, 4
VMEM = 16 << 20


def along_row(array, size, first, second):
    pairs = [((row * 2 + core), (row + step) % size * 2 + core) for row in range(size) for core, step in enumerate((first, second))]
    return lax.ppermute(array, ("row", "col"), pairs)


def travel(array, first, second):
    pairs = []
    for core, step in enumerate((first, second)):
        if step is not None:
            for z in range(Z):
                for y in range(Y):
                    target = (z + step[0]) % Z * Y + (y + step[1]) % Y
                    pairs.append(((core * Z + z) * Y + y, core * Z * Y + target))
    return lax.ppermute(array, ("col", "depth"), pairs)


def swap(array):
    return lax.ppermute(array, "col", [(0, 1), (1, 0)])


def padded(blocks, rows):
    parts = blocks.reshape(-1, rows, blocks.shape[-1])
    return jnp.pad(parts, ((0, 0), (0, -rows % 8), (0, 0)))


def gather(block, height, amplitudes, rows, multiply_first):
    count = amplitudes.shape[0]
    along, back = ((0, 1), (1, 0)), ((0, -1), (-1, 0))
    up, down = ((1, 0), (0, 1)), ((-1, 0), (0, -1))
    near = along_row(amplitudes, rows, 1, -1)
    a1 = travel(block, *along)
    b1 = travel(block, *back)
    a2 = travel(a1, *along)
    pack = jnp.concatenate([block, a1, b1, a2])
    b2 = travel(b1, None, back[1])
    a3 = travel(a2, None, along[1])
    own, near, b2, a3 = lax.optimization_barrier((amplitudes, near, b2, a3))
    other = along_row(own, rows, -1, 1)
    b3 = travel(b2, None, back[1])
    a4 = travel(a3, None, along[1])
    near, b3, a4 = lax.optimization_barrier((near, b3, a4))
    far_low = along_row(near[: count // 2], rows, 1, -1)
    rest = jnp.concatenate([b2, a3, b3, a4])
    u1, d1 = travel(pack, *up), travel(pack, *down)
    u2, d2 = travel(u1, *up), travel(d1, down[0], None)
    far_high = along_row(other[count // 2 :], rows, -1, 1)
    u2, d2, far_low, far_high = lax.optimization_barrier((u2, d2, far_low, far_high))
    first = lax.axis_index("col") == 0
    kept = jnp.where(first, d2, rest)
    u3, d3 = travel(jnp.where(first, u2, rest), *up), travel(kept, *down)
    factors = arrange(amplitudes, near, other, far_low, far_high, rows, height, [20, 8, 4])
    early = [pack, u1, d1, u2, kept]
    total = multiply_first(factors[0], early + [swap(piece) for piece in early])
    u3, d3, total = lax.optimization_barrier((u3, d3, total))
    u4, d4 = travel(u3[:2], *up), travel(d3[2:], *down)
    return factors[1:], total, [u3, d3, swap(u3), swap(d3)], [u4, d4, swap(u4), swap(d4)]


def arrange(own, near, other, far_low, far_high, rows, height, cuts):
    width = own.shape[1]
    count = own.shape[0] // height
    full = height + -height % 8

    def kernel(own_ref, near_ref, other_ref, low_ref, high_ref, *refs):
        out_refs, held = refs[:-1], refs[-1]
        x, core, depth = (lax.axis_index(name) for name in ("row", "col", "depth"))
        z, y = depth // Y, lax.rem(depth, Y)
        held[:, :, height:, :] = jnp.zeros((2, Z * Y, full - height, width), held.dtype)
        steps = rows - 1 + core * (2 - rows), 1 + core * (rows - 2)
        sources = [(own_ref, 0, 0), (near_ref, steps[0], 0), (other_ref, steps[1], 0), (low_ref, 2, 0), (high_ref, 2, count // 2)]
        for ref, step, start in sources:
            block_row = lax.rem(x + step, rows)
            half = block_row // (rows // 2)
            for i in range(ref.shape[0] // height):
                there = lax.rem(block_row, rows // 2) * count + start + i
                dz = lax.rem(there // Y - z + Z, Z)
                dy = lax.rem((start + i) % Y - y + Y, Y)
                oz = jnp.where(dz < Z // 2, 2 * dz, 2 * (Z - dz) - 1)
                oy = jnp.where(dy < Y // 2, 2 * dy, 2 * (Y - dy) - 1)
                place = jnp.where(half == 0, oz * Y + oy, oz // Y * (Y * Y) + oy * Y + lax.rem(oz, Y))
                held[lax.rem(half + core, 2), place, pl.ds(0, height), :] = ref[pl.ds(i * height, height), :]
        for side in range(2):
            at = 0
            for out_ref, blocks in zip(out_refs, cuts):
                part = held[side, pl.ds(at, blocks)].reshape(blocks * full, width)
                out_ref[side] = part.T
                at += blocks

    size = 2 * own.size * rows
    return pl.pallas_call(
        kernel,
        out_shape=[jax.ShapeDtypeStruct((2, width, blocks * full), own.dtype) for blocks in cuts],
        scratch_shapes=[pltpu.VMEM((2, Z * Y, full, width), own.dtype)],
        compiler_params=pltpu.CompilerParams(vmem_limit_bytes=VMEM),
        cost_estimate=pl.CostEstimate(flops=0, bytes_accessed=2 * size, transcendentals=0),
        name="arrange",
    )(own, near, other, far_low, far_high)


def products(factor_ref, piece_refs, start, width):
    share = 0.0
    count = len(piece_refs) // 2
    for side in range(2):
        part = jnp.concatenate([ref[:, pl.ds(start, width)] for ref in piece_refs[side * count :][:count]])
        share += jnp.dot(factor_ref[side], part, preferred_element_type=jnp.float32)
    return share


def multiply(body, shape, factor, pieces, *operands, **options):
    columns = pieces[0].shape[-1]
    flops = 4 * factor.shape[1] * factor.shape[2] * columns
    return pl.pallas_call(
        body,
        out_shape=jax.ShapeDtypeStruct(shape, jnp.float32),
        compiler_params=pltpu.CompilerParams(vmem_limit_bytes=VMEM),
        cost_estimate=pl.CostEstimate(flops=flops, bytes_accessed=flops // 512, transcendentals=0),
        **options,
    )(*operands, factor, *[piece.reshape(-1, columns) for piece in pieces])


def tiles(columns, tile=256):
    return [(start, min(tile, columns - start)) for start in range(0, columns, tile)]


def first_products(factor, pieces):
    def body(factor_ref, *refs):
        for start, width in tiles(refs[-1].shape[1]):
            refs[-1][:, pl.ds(start, width)] = products(factor_ref, refs[:-1], start, width)

    return multiply(body, (factor.shape[1], pieces[0].shape[-1]), factor, pieces, name="first")


def more_products(residual, total, factor, pieces):
    def body(residual_ref, total_ref, factor_ref, *refs):
        for start, width in tiles(refs[-1].shape[0]):
            part = pl.ds(start, width)
            share = total_ref[:, part] + products(factor_ref, refs[:-1], start, width)
            refs[-1][part, :] = residual_ref[part, :] + share.T

    return multiply(body, residual.shape, factor, pieces, residual, total, name="more")


def last_products(total, factor, pieces):
    parts = tiles(total.shape[0])

    def body(total_ref, factor_ref, *refs):
        *piece_refs, out_ref, held, sems = refs
        copies = []
        for number, (start, width) in enumerate(parts):
            part = pl.ds(start, width)
            held[part, :] = total_ref[part, :] + products(factor_ref, piece_refs, start, width).T
            copies.append(pltpu.make_async_copy(held.at[part], out_ref.at[part], sems.at[number]))
            copies[-1].start()
        for copy in copies:
            copy.wait()

    return multiply(
        body,
        total.shape,
        factor,
        pieces,
        total,
        out_specs=pl.BlockSpec(memory_space=pl.ANY),
        scratch_shapes=[pltpu.VMEM(total.shape, jnp.float32), pltpu.SemaphoreType.DMA((len(parts),))],
        name="last",
    )


def solution(mesh):
    rows = mesh.shape["row"]

    def per_device(residual_in, integrals, amplitudes):
        height = integrals.shape[1]
        block = padded(integrals.T, height)
        factors, total, more, last = gather(block, height, amplitudes, rows, first_products)
        total = more_products(residual_in.T, total, factors[0], more)
        return last_products(total, factors[1], last).T

    placed = (P(("col", "depth"), "row"), P("row", ("col", "depth")), P("row", ("col", "depth")))
    return jax.shard_map(
        per_device, mesh=mesh, in_specs=placed, out_specs=P(("col", "depth"), "row"), check_vma=False
    )
```

```python
import jax
import jax.numpy as jnp
from jax import lax
from jax.experimental import pallas as pl
from jax.experimental.pallas import tpu as pltpu
from jax.sharding import PartitionSpec as P

Z, Y = 8, 4
VMEM = 16 << 20


def along_row(array, size, first, second):
    pairs = [((row * 2 + core), (row + step) % size * 2 + core) for row in range(size) for core, step in enumerate((first, second))]
    return lax.ppermute(array, ("row", "col"), pairs)


def travel(array, first, second):
    pairs = []
    for core, step in enumerate((first, second)):
        if step is not None:
            for z in range(Z):
                for y in range(Y):
                    target = (z + step[0]) % Z * Y + (y + step[1]) % Y
                    pairs.append(((core * Z + z) * Y + y, core * Z * Y + target))
    return lax.ppermute(array, ("col", "depth"), pairs)


def swap(array):
    return lax.ppermute(array, "col", [(0, 1), (1, 0)])


def padded(blocks, rows):
    parts = blocks.reshape(-1, rows, blocks.shape[-1])
    return jnp.pad(parts, ((0, 0), (0, -rows % 8), (0, 0)))


def gather(block, height, amplitudes, rows, multiply_first):
    cut = amplitudes.shape[0] // 4 * 3
    along, back = ((0, 1), (1, 0)), ((0, -1), (-1, 0))
    up, down = ((1, 0), (0, 1)), ((-1, 0), (0, -1))
    near = along_row(amplitudes, rows, 1, -1)
    a1 = travel(block, *along)
    b1 = travel(block, *back)
    a2 = travel(a1, *along)
    pack = jnp.concatenate([block, a1, b1, a2])
    b2 = travel(b1, None, back[1])
    a3 = travel(a2, None, along[1])
    own, near, b2, a3 = lax.optimization_barrier((amplitudes, near, b2, a3))
    other = along_row(own, rows, -1, 1)
    b3 = travel(b2, None, back[1])
    a4 = travel(a3, None, along[1])
    far_low = along_row(near[:cut], rows, 1, -1)
    rest = jnp.concatenate([b2, a3, b3, a4])
    u1, d1 = travel(pack, *up), travel(pack, *down)
    u2, d2 = travel(u1, *up), travel(d1, down[0], None)
    far_high = along_row(other[cut:], rows, -1, 1)
    u2, d2, far_low, far_high = lax.optimization_barrier((u2, d2, far_low, far_high))
    first = lax.axis_index("col") == 0
    kept = jnp.where(first, d2, rest)
    u3, d3 = travel(jnp.where(first, u2, rest), *up), travel(kept, *down)
    early = [pack, u1, d1, u2, kept]
    early = early + [swap(piece) for piece in early]
    factors = arrange(amplitudes, near, other, far_low, far_high, rows, height, [20, 8, 4])
    u3, d3, factors, early = lax.optimization_barrier((u3, d3, factors, early))
    u4, d4 = travel(u3[:2], *up), travel(d3[2:], *down)
    more = [u3, d3, swap(u3), swap(d3)]
    total = multiply_first(factors[0], early)
    u4, d4, total = lax.optimization_barrier((u4, d4, total))
    return factors[1:], total, more, [u4, d4, swap(u4), swap(d4)]


def arrange(own, near, other, far_low, far_high, rows, height, cuts):
    width = own.shape[1]
    count = own.shape[0] // height
    full = height + -height % 8

    def kernel(own_ref, near_ref, other_ref, low_ref, high_ref, *refs):
        out_refs, held = refs[:-1], refs[-1]
        x, core, depth = (lax.axis_index(name) for name in ("row", "col", "depth"))
        z, y = depth // Y, lax.rem(depth, Y)
        held[:, :, height:, :] = jnp.zeros((2, Z * Y, full - height, width), held.dtype)
        steps = rows - 1 + core * (2 - rows), 1 + core * (rows - 2)
        sources = [(own_ref, 0, 0), (near_ref, steps[0], 0), (other_ref, steps[1], 0), (low_ref, 2, 0), (high_ref, 2, far_low.shape[0] // height)]
        for ref, step, start in sources:
            block_row = lax.rem(x + step, rows)
            half = block_row // (rows // 2)
            for i in range(ref.shape[0] // height):
                there = lax.rem(block_row, rows // 2) * count + start + i
                dz = lax.rem(there // Y - z + Z, Z)
                dy = lax.rem((start + i) % Y - y + Y, Y)
                oz = jnp.where(dz < Z // 2, 2 * dz, 2 * (Z - dz) - 1)
                oy = jnp.where(dy < Y // 2, 2 * dy, 2 * (Y - dy) - 1)
                place = jnp.where(half == 0, oz * Y + oy, oz // Y * (Y * Y) + oy * Y + lax.rem(oz, Y))
                held[lax.rem(half + core, 2), place, pl.ds(0, height), :] = ref[pl.ds(i * height, height), :]
        for side in range(2):
            at = 0
            for out_ref, blocks in zip(out_refs, cuts):
                part = held[side, pl.ds(at, blocks)].reshape(blocks * full, width)
                out_ref[side] = part.T
                at += blocks

    size = 2 * own.size * rows
    return pl.pallas_call(
        kernel,
        out_shape=[jax.ShapeDtypeStruct((2, width, blocks * full), own.dtype) for blocks in cuts],
        scratch_shapes=[pltpu.VMEM((2, Z * Y, full, width), own.dtype)],
        compiler_params=pltpu.CompilerParams(vmem_limit_bytes=VMEM),
        cost_estimate=pl.CostEstimate(flops=0, bytes_accessed=2 * size, transcendentals=0),
        name="arrange",
    )(own, near, other, far_low, far_high)


def products(factor_ref, piece_refs, start, width):
    share = 0.0
    count = len(piece_refs) // 2
    for side in range(2):
        part = jnp.concatenate([ref[:, pl.ds(start, width)] for ref in piece_refs[side * count :][:count]])
        share += jnp.dot(factor_ref[side], part, preferred_element_type=jnp.float32)
    return share


def multiply(body, shape, factor, pieces, *operands, **options):
    columns = pieces[0].shape[-1]
    flops = 4 * factor.shape[1] * factor.shape[2] * columns
    return pl.pallas_call(
        body,
        out_shape=jax.ShapeDtypeStruct(shape, jnp.float32),
        compiler_params=pltpu.CompilerParams(vmem_limit_bytes=VMEM),
        cost_estimate=pl.CostEstimate(flops=flops, bytes_accessed=flops // 512, transcendentals=0),
        **options,
    )(*operands, factor, *[piece.reshape(-1, columns) for piece in pieces])


def tiles(columns, tile=256):
    return [(start, min(tile, columns - start)) for start in range(0, columns, tile)]


def first_products(factor, pieces):
    def body(factor_ref, *refs):
        for start, width in tiles(refs[-1].shape[1]):
            refs[-1][:, pl.ds(start, width)] = products(factor_ref, refs[:-1], start, width)

    return multiply(body, (factor.shape[1], pieces[0].shape[-1]), factor, pieces, name="first")


def more_products(residual, total, factor, pieces):
    def body(residual_ref, total_ref, factor_ref, *refs):
        for start, width in tiles(refs[-1].shape[0]):
            part = pl.ds(start, width)
            share = total_ref[:, part] + products(factor_ref, refs[:-1], start, width)
            refs[-1][part, :] = residual_ref[part, :] + share.T

    return multiply(body, residual.shape, factor, pieces, residual, total, name="more")


def last_products(total, factor, pieces):
    parts = tiles(total.shape[0])

    def body(total_ref, factor_ref, *refs):
        *piece_refs, out_ref, held, sems = refs
        copies = []
        for number, (start, width) in enumerate(parts):
            part = pl.ds(start, width)
            held[part, :] = total_ref[part, :] + products(factor_ref, piece_refs, start, width).T
            copies.append(pltpu.make_async_copy(held.at[part], out_ref.at[part], sems.at[number]))
            copies[-1].start()
        for copy in copies:
            copy.wait()

    return multiply(
        body,
        total.shape,
        factor,
        pieces,
        total,
        out_specs=pl.BlockSpec(memory_space=pl.ANY),
        scratch_shapes=[pltpu.VMEM(total.shape, jnp.float32), pltpu.SemaphoreType.DMA((len(parts),))],
        name="last",
    )


def solution(mesh):
    rows = mesh.shape["row"]

    def per_device(residual_in, integrals, amplitudes):
        height = integrals.shape[1]
        block = padded(integrals.T, height)
        factors, total, more, last = gather(block, height, amplitudes, rows, first_products)
        total = more_products(residual_in.T, total, factors[0], more)
        return last_products(total, factors[1], last).T

    placed = (P(("col", "depth"), "row"), P("row", ("col", "depth")), P("row", ("col", "depth")))
    return jax.shard_map(
        per_device, mesh=mesh, in_specs=placed, out_specs=P(("col", "depth"), "row"), check_vma=False
    )
```

```python
import jax
import jax.numpy as jnp
from jax import lax
from jax.experimental import pallas as pl
from jax.experimental.pallas import tpu as pltpu
from jax.sharding import PartitionSpec as P

Z, Y = 8, 4
VMEM = 16 << 20


def along_row(array, size, first, second):
    pairs = [((row * 2 + core), (row + step) % size * 2 + core) for row in range(size) for core, step in enumerate((first, second))]
    return lax.ppermute(array, ("row", "col"), pairs)


def travel(array, first, second):
    pairs = []
    for core, step in enumerate((first, second)):
        if step is not None:
            for z in range(Z):
                for y in range(Y):
                    target = (z + step[0]) % Z * Y + (y + step[1]) % Y
                    pairs.append(((core * Z + z) * Y + y, core * Z * Y + target))
    return lax.ppermute(array, ("col", "depth"), pairs)


def swap(array):
    return lax.ppermute(array, "col", [(0, 1), (1, 0)])


def padded(blocks, rows):
    parts = blocks.reshape(-1, rows, blocks.shape[-1])
    return jnp.pad(parts, ((0, 0), (0, -rows % 8), (0, 0)))


def gather(block, height, amplitudes, rows, multiply_first):
    cut = amplitudes.shape[0] // 4 * 3
    along, back = ((0, 1), (1, 0)), ((0, -1), (-1, 0))
    up, down = ((1, 0), (0, 1)), ((-1, 0), (0, -1))
    near = along_row(amplitudes, rows, 1, -1)
    a1 = travel(block, *along)
    b1 = travel(block, *back)
    a2 = travel(a1, *along)
    pack = jnp.concatenate([block, a1, b1, a2])
    b2 = travel(b1, None, back[1])
    a3 = travel(a2, None, along[1])
    own, near, b2, a3 = lax.optimization_barrier((amplitudes, near, b2, a3))
    other = along_row(own, rows, -1, 1)
    b3 = travel(b2, None, back[1])
    a4 = travel(a3, None, along[1])
    far_low = along_row(near[:cut], rows, 1, -1)
    rest = jnp.concatenate([b2, a3, b3, a4])
    u1, d1 = travel(pack, *up), travel(pack, *down)
    u2, d2 = travel(u1, *up), travel(d1, down[0], None)
    u2, d2, other, far_low = lax.optimization_barrier((u2, d2, other, far_low))
    far_high = along_row(other[cut:], rows, -1, 1)
    first = lax.axis_index("col") == 0
    kept = jnp.where(first, d2, rest)
    u3, d3 = travel(jnp.where(first, u2, rest), *up), travel(kept, *down)
    early = [pack, u1, d1, u2, kept]
    early = early + [swap(piece) for piece in early]
    factors = arrange(amplitudes, near, other, far_low, far_high, rows, height, [20, 8, 4])
    u3, d3, factors, early = lax.optimization_barrier((u3, d3, factors, early))
    u4, d4 = travel(u3[:2], *up), travel(d3[2:], *down)
    more = [u3, d3, swap(u3), swap(d3)]
    total = multiply_first(factors[0], early)
    u4, d4, total = lax.optimization_barrier((u4, d4, total))
    return factors[1:], total, more, [u4, d4, swap(u4), swap(d4)]


def arrange(own, near, other, far_low, far_high, rows, height, cuts):
    width = own.shape[1]
    count = own.shape[0] // height
    full = height + -height % 8

    def kernel(own_ref, near_ref, other_ref, low_ref, high_ref, *refs):
        out_refs, held = refs[:-1], refs[-1]
        x, core, depth = (lax.axis_index(name) for name in ("row", "col", "depth"))
        z, y = depth // Y, lax.rem(depth, Y)
        held[:, :, height:, :] = jnp.zeros((2, Z * Y, full - height, width), held.dtype)
        steps = rows - 1 + core * (2 - rows), 1 + core * (rows - 2)
        sources = [(own_ref, 0, 0), (near_ref, steps[0], 0), (other_ref, steps[1], 0), (low_ref, 2, 0), (high_ref, 2, far_low.shape[0] // height)]
        for ref, step, start in sources:
            block_row = lax.rem(x + step, rows)
            half = block_row // (rows // 2)
            for i in range(ref.shape[0] // height):
                there = lax.rem(block_row, rows // 2) * count + start + i
                dz = lax.rem(there // Y - z + Z, Z)
                dy = lax.rem((start + i) % Y - y + Y, Y)
                oz = jnp.where(dz < Z // 2, 2 * dz, 2 * (Z - dz) - 1)
                oy = jnp.where(dy < Y // 2, 2 * dy, 2 * (Y - dy) - 1)
                place = jnp.where(half == 0, oz * Y + oy, oz // Y * (Y * Y) + oy * Y + lax.rem(oz, Y))
                held[lax.rem(half + core, 2), place, pl.ds(0, height), :] = ref[pl.ds(i * height, height), :]
        for side in range(2):
            at = 0
            for out_ref, blocks in zip(out_refs, cuts):
                part = held[side, pl.ds(at, blocks)].reshape(blocks * full, width)
                out_ref[side] = part.T
                at += blocks

    size = 2 * own.size * rows
    return pl.pallas_call(
        kernel,
        out_shape=[jax.ShapeDtypeStruct((2, width, blocks * full), own.dtype) for blocks in cuts],
        scratch_shapes=[pltpu.VMEM((2, Z * Y, full, width), own.dtype)],
        compiler_params=pltpu.CompilerParams(vmem_limit_bytes=VMEM),
        cost_estimate=pl.CostEstimate(flops=0, bytes_accessed=2 * size, transcendentals=0),
        name="arrange",
    )(own, near, other, far_low, far_high)


def products(factor_ref, piece_refs, start, width):
    share = 0.0
    count = len(piece_refs) // 2
    for side in range(2):
        part = jnp.concatenate([ref[:, pl.ds(start, width)] for ref in piece_refs[side * count :][:count]])
        share += jnp.dot(factor_ref[side], part, preferred_element_type=jnp.float32)
    return share


def multiply(body, shape, factor, pieces, *operands, **options):
    columns = pieces[0].shape[-1]
    flops = 4 * factor.shape[1] * factor.shape[2] * columns
    return pl.pallas_call(
        body,
        out_shape=jax.ShapeDtypeStruct(shape, jnp.float32),
        compiler_params=pltpu.CompilerParams(vmem_limit_bytes=VMEM),
        cost_estimate=pl.CostEstimate(flops=flops, bytes_accessed=flops // 512, transcendentals=0),
        **options,
    )(*operands, factor, *[piece.reshape(-1, columns) for piece in pieces])


def tiles(columns, tile=256):
    return [(start, min(tile, columns - start)) for start in range(0, columns, tile)]


def first_products(factor, pieces):
    def body(factor_ref, *refs):
        for start, width in tiles(refs[-1].shape[1]):
            refs[-1][:, pl.ds(start, width)] = products(factor_ref, refs[:-1], start, width)

    return multiply(body, (factor.shape[1], pieces[0].shape[-1]), factor, pieces, name="first")


def more_products(residual, total, factor, pieces):
    def body(residual_ref, total_ref, factor_ref, *refs):
        for start, width in tiles(refs[-1].shape[0]):
            part = pl.ds(start, width)
            share = total_ref[:, part] + products(factor_ref, refs[:-1], start, width)
            refs[-1][part, :] = residual_ref[part, :] + share.T

    return multiply(body, residual.shape, factor, pieces, residual, total, name="more")


def last_products(total, factor, pieces):
    parts = tiles(total.shape[0])

    def body(total_ref, factor_ref, *refs):
        *piece_refs, out_ref, held, sems = refs
        copies = []
        for number, (start, width) in enumerate(parts):
            part = pl.ds(start, width)
            held[part, :] = total_ref[part, :] + products(factor_ref, piece_refs, start, width).T
            copies.append(pltpu.make_async_copy(held.at[part], out_ref.at[part], sems.at[number]))
            copies[-1].start()
        for copy in copies:
            copy.wait()

    return multiply(
        body,
        total.shape,
        factor,
        pieces,
        total,
        out_specs=pl.BlockSpec(memory_space=pl.ANY),
        scratch_shapes=[pltpu.VMEM(total.shape, jnp.float32), pltpu.SemaphoreType.DMA((len(parts),))],
        name="last",
    )


def solution(mesh):
    rows = mesh.shape["row"]

    def per_device(residual_in, integrals, amplitudes):
        height = integrals.shape[1]
        block = padded(integrals.T, height)
        factors, total, more, last = gather(block, height, amplitudes, rows, first_products)
        total = more_products(residual_in.T, total, factors[0], more)
        return last_products(total, factors[1], last).T

    placed = (P(("col", "depth"), "row"), P("row", ("col", "depth")), P("row", ("col", "depth")))
    return jax.shard_map(
        per_device, mesh=mesh, in_specs=placed, out_specs=P(("col", "depth"), "row"), check_vma=False
    )
```

```python
import jax
import jax.numpy as jnp
from jax import lax
from jax.experimental import pallas as pl
from jax.experimental.pallas import tpu as pltpu
from jax.sharding import PartitionSpec as P

Z, Y = 8, 4
VMEM = 16 << 20
TIE = 1


def along_row(array, size, first, second):
    pairs = [((row * 2 + core), (row + step) % size * 2 + core) for row in range(size) for core, step in enumerate((first, second))]
    return lax.ppermute(array, ("row", "col"), pairs)


def travel(array, first, second):
    pairs = []
    for core, step in enumerate((first, second)):
        if step is not None:
            for z in range(Z):
                for y in range(Y):
                    target = (z + step[0]) % Z * Y + (y + step[1]) % Y
                    pairs.append(((core * Z + z) * Y + y, core * Z * Y + target))
    return lax.ppermute(array, ("col", "depth"), pairs)


def swap(array):
    return lax.ppermute(array, "col", [(0, 1), (1, 0)])


def padded(blocks, rows):
    parts = blocks.reshape(-1, rows, blocks.shape[-1])
    return jnp.pad(parts, ((0, 0), (0, -rows % 8), (0, 0)))


def ladder(block, height, amplitudes, rows, residual):
    cut = amplitudes.shape[0] // 4 * 3
    along, back = ((0, 1), (1, 0)), ((0, -1), (-1, 0))
    up, down = ((1, 0), (0, 1)), ((-1, 0), (0, -1))
    near = along_row(amplitudes, rows, 1, -1)
    a1 = travel(block, *along)
    b1 = travel(block, *back)
    a2 = travel(block, (0, 2), (2, 0))
    pack = jnp.concatenate([block, a1, b1, a2])
    b2 = travel(b1, None, back[1])
    a3 = travel(a2, None, along[1])
    own, near, b2, a3 = lax.optimization_barrier((amplitudes, near, b2, a3))
    other = along_row(own, rows, -1, 1)
    b3 = travel(b2, None, back[1])
    a4 = travel(a3, None, along[1])
    far_low = along_row(near[:cut], rows, 1, -1)
    rest = jnp.concatenate([b2, a3, b3, a4])
    u1, d1 = travel(pack, *up), travel(pack, *down)
    u2, d2 = travel(u1, *up), travel(d1, down[0], None)
    u2, d2, other, far_low = lax.optimization_barrier((u2, d2, other, far_low))
    first = lax.axis_index("col") == 0
    kept = jnp.where(first, d2, rest)
    u3, d3 = travel(jnp.where(first, u2, rest), *up), travel(kept, *down)
    theirs = [swap(piece) for piece in (pack, u1, d1, u2, kept)]
    other, theirs[TIE] = lax.optimization_barrier((other, theirs[TIE]))
    far_high = along_row(other[cut:], rows, -1, 1)
    own_factors, their_factors = arrange(amplitudes, near, other, far_low, far_high, rows, height)
    total = first_products([own_factors[0], their_factors[0]], [[pack], theirs[:1]])
    u3, d3, total = lax.optimization_barrier((u3, d3, total))
    u4, d4 = travel(u3[:2], *up), travel(d3[2:], *down)
    total = second_products(total, [own_factors[1], their_factors[1]], [[u1, d1, u2, kept], theirs[1:]])
    theirs = [swap(u3), swap(d3)]
    u4, d4, total = lax.optimization_barrier((u4, d4, total))
    total = more_products(residual, total, [own_factors[2], their_factors[2]], [[u3, d3, u4, d4], theirs])
    return last_products(total, their_factors[3], [swap(u4), swap(d4)])


def arrange(own, near, other, far_low, far_high, rows, height):
    cuts = [(0, blocks) for blocks in (4, 16, 12)] + [(1, blocks) for blocks in (4, 16, 8, 4)]
    width = own.shape[1]
    count = own.shape[0] // height
    full = height + -height % 8

    def kernel(own_ref, near_ref, other_ref, low_ref, high_ref, *refs):
        out_refs, held = refs[:-1], refs[-1]
        x, core, depth = (lax.axis_index(name) for name in ("row", "col", "depth"))
        z, y = depth // Y, lax.rem(depth, Y)
        held[:, :, height:, :] = jnp.zeros((2, Z * Y, full - height, width), held.dtype)
        steps = rows - 1 + core * (2 - rows), 1 + core * (rows - 2)
        sources = [(own_ref, 0, 0), (near_ref, steps[0], 0), (other_ref, steps[1], 0), (low_ref, 2, 0), (high_ref, 2, far_low.shape[0] // height)]
        for ref, step, start in sources:
            block_row = lax.rem(x + step, rows)
            half = block_row // (rows // 2)
            for i in range(ref.shape[0] // height):
                there = lax.rem(block_row, rows // 2) * count + start + i
                dz = lax.rem(there // Y - z + Z, Z)
                dy = lax.rem((start + i) % Y - y + Y, Y)
                oz = jnp.where(dz < Z // 2, 2 * dz, 2 * (Z - dz) - 1)
                oy = jnp.where(dy < Y // 2, 2 * dy, 2 * (Y - dy) - 1)
                place = jnp.where(half == 0, oz * Y + oy, oz // Y * (Y * Y) + oy * Y + lax.rem(oz, Y))
                held[lax.rem(half + core, 2), place, pl.ds(0, height), :] = ref[pl.ds(i * height, height), :]
        at = [0, 0]
        for out_ref, (side, blocks) in zip(out_refs, cuts):
            part = held[side, pl.ds(at[side], blocks)].reshape(blocks * full, width)
            out_ref[...] = part if out_ref is out_refs[-1] else part.T
            at[side] += blocks

    size = 2 * own.size * rows
    shapes = [(width, blocks * full) for _, blocks in cuts]
    shapes[-1] = shapes[-1][::-1]
    factors = pl.pallas_call(
        kernel,
        out_shape=[jax.ShapeDtypeStruct(shape, own.dtype) for shape in shapes],
        scratch_shapes=[pltpu.VMEM((2, Z * Y, full, width), own.dtype)],
        compiler_params=pltpu.CompilerParams(vmem_limit_bytes=VMEM),
        cost_estimate=pl.CostEstimate(flops=0, bytes_accessed=2 * size, transcendentals=0),
        name="arrange",
    )(own, near, other, far_low, far_high)
    return factors[:3], factors[3:]


def products(refs, counts, start, width):
    share, at = 0.0, 0
    for count in counts:
        part = jnp.concatenate([ref[:, pl.ds(start, width)] for ref in refs[at + 1 : at + 1 + count]])
        share += jnp.dot(refs[at][...], part, preferred_element_type=jnp.float32)
        at += count + 1
    return share


def multiply(body, shape, factors, pieces, *operands, **options):
    columns = pieces[0][0].shape[-1]
    flops = 2 * sum(factor.size for factor in factors) * columns
    flat = []
    for factor, group in zip(factors, pieces):
        flat += [factor, *[piece.reshape(-1, columns) for piece in group]]
    return pl.pallas_call(
        body,
        out_shape=jax.ShapeDtypeStruct(shape, jnp.float32),
        compiler_params=pltpu.CompilerParams(vmem_limit_bytes=VMEM),
        cost_estimate=pl.CostEstimate(flops=flops, bytes_accessed=flops // 512, transcendentals=0),
        **options,
    )(*operands, *flat)


def tiles(columns, tile=256):
    return [(start, min(tile, columns - start)) for start in range(0, columns, tile)]


def first_products(factors, pieces):
    counts = [len(group) for group in pieces]

    def body(*refs):
        for start, width in tiles(refs[-1].shape[1]):
            refs[-1][:, pl.ds(start, width)] = products(refs, counts, start, width)

    return multiply(body, (factors[0].shape[0], pieces[0][0].shape[-1]), factors, pieces, name="first")


def second_products(total, factors, pieces):
    counts = [len(group) for group in pieces]

    def body(total_ref, *refs):
        for start, width in tiles(refs[-1].shape[1]):
            part = pl.ds(start, width)
            refs[-1][:, part] = total_ref[:, part] + products(refs, counts, start, width)

    return multiply(body, total.shape, factors, pieces, total, name="second")


def more_products(residual, total, factors, pieces):
    counts = [len(group) for group in pieces]

    def body(residual_ref, total_ref, *refs):
        for start, width in tiles(refs[-1].shape[0]):
            part = pl.ds(start, width)
            share = total_ref[:, part] + products(refs, counts, start, width)
            refs[-1][part, :] = residual_ref[part, :] + share.T

    return multiply(body, residual.shape, factors, pieces, residual, total, name="more")


def last_products(total, factor, pieces):
    parts = tiles(total.shape[0])

    def body(total_ref, factor_ref, *refs):
        *piece_refs, out_ref, held, sems = refs
        copies = []
        for number, (start, width) in enumerate(parts):
            part = pl.ds(start, width)
            piece = jnp.concatenate([ref[:, part] for ref in piece_refs])
            share = lax.dot_general(piece, factor_ref[...], (((0,), (0,)), ((), ())), preferred_element_type=jnp.float32)
            held[part, :] = total_ref[part, :] + share
            copies.append(pltpu.make_async_copy(held.at[part], out_ref.at[part], sems.at[number]))
            copies[-1].start()
        for copy in copies:
            copy.wait()

    return multiply(
        body,
        total.shape,
        [factor],
        [pieces],
        total,
        out_specs=pl.BlockSpec(memory_space=pl.ANY),
        scratch_shapes=[pltpu.VMEM(total.shape, jnp.float32), pltpu.SemaphoreType.DMA((len(parts),))],
        name="last",
    )


def solution(mesh):
    rows = mesh.shape["row"]

    def per_device(residual_in, integrals, amplitudes):
        height = integrals.shape[1]
        block = padded(integrals.T, height)
        return ladder(block, height, amplitudes, rows, residual_in.T).T

    placed = (P(("col", "depth"), "row"), P("row", ("col", "depth")), P("row", ("col", "depth")))
    return jax.shard_map(
        per_device, mesh=mesh, in_specs=placed, out_specs=P(("col", "depth"), "row"), check_vma=False
    )
```

```python
import jax
import jax.numpy as jnp
from jax import lax
from jax.experimental import pallas as pl
from jax.experimental.pallas import tpu as pltpu
from jax.sharding import PartitionSpec as P

Z, Y = 8, 4
VMEM = 16 << 20


def along_row(array, size, first, second):
    pairs = [((row * 2 + core), (row + step) % size * 2 + core) for row in range(size) for core, step in enumerate((first, second))]
    return lax.ppermute(array, ("row", "col"), pairs)


def travel(array, first, second):
    pairs = []
    for core, step in enumerate((first, second)):
        if step is not None:
            for z in range(Z):
                for y in range(Y):
                    target = (z + step[0]) % Z * Y + (y + step[1]) % Y
                    pairs.append(((core * Z + z) * Y + y, core * Z * Y + target))
    return lax.ppermute(array, ("col", "depth"), pairs)


def swap(array):
    return lax.ppermute(array, "col", [(0, 1), (1, 0)])


def padded(blocks, rows):
    parts = blocks.reshape(-1, rows, blocks.shape[-1])
    return jnp.pad(parts, ((0, 0), (0, -rows % 8), (0, 0)))


def ladder(block, height, amplitudes, rows, residual):
    along, back = ((0, 1), (1, 0)), ((0, -1), (-1, 0))
    up, down = ((1, 0), (0, 1)), ((-1, 0), (0, -1))
    near = along_row(amplitudes, rows, 1, -1)
    a1 = travel(block, *along)
    b1 = travel(block, *back)
    a2 = travel(block, (0, 2), (2, 0))
    pack = jnp.concatenate([block, a1, b1, a2])
    b2 = travel(b1, None, back[1])
    a3 = travel(a2, None, along[1])
    own, near, b2, a3 = lax.optimization_barrier((amplitudes, near, b2, a3))
    other = along_row(own, rows, -1, 1)
    b3 = travel(b2, None, back[1])
    a4 = travel(a3, None, along[1])
    far = along_row(near, rows, 1, -1)
    rest = jnp.concatenate([b2, a3, b3, a4])
    u1, d1 = travel(pack, *up), travel(pack, *down)
    u2, d2 = travel(u1, *up), travel(d1, down[0], None)
    u2, d2, other, far = lax.optimization_barrier((u2, d2, other, far))
    first = lax.axis_index("col") == 0
    kept = jnp.where(first, d2, rest)
    u3, d3 = travel(jnp.where(first, u2, rest), *up), travel(kept, *down)
    theirs = [swap(piece) for piece in (pack, u1, d1, u2, kept)]
    own_factors, their_factors = arrange(amplitudes, near, other, far, rows, height)
    total = first_products([own_factors[0], their_factors[0]], [[pack, u1, d1], theirs[:3]])
    u3, d3, total = lax.optimization_barrier((u3, d3, total))
    u4, d4 = travel(u3[:2], *up), travel(d3[2:], *down)
    total = second_products(total, [own_factors[1], their_factors[1]], [[u2, kept], theirs[3:]])
    theirs = [swap(u3), swap(d3)]
    u4, d4, total = lax.optimization_barrier((u4, d4, total))
    total = more_products(residual, total, [own_factors[2], their_factors[2]], [[u3, d3, u4, d4], theirs])
    return last_products(total, their_factors[3], [swap(u4), swap(d4)])


def arrange(own, near, other, far, rows, height):
    cuts = [(0, blocks) for blocks in (12, 8, 12)] + [(1, blocks) for blocks in (12, 8, 8, 4)]
    width = own.shape[1]
    count = own.shape[0] // height
    full = height + -height % 8

    def kernel(own_ref, near_ref, other_ref, far_ref, *refs):
        out_refs, held = refs[:-1], refs[-1]
        x, core, depth = (lax.axis_index(name) for name in ("row", "col", "depth"))
        z, y = depth // Y, lax.rem(depth, Y)
        held[:, :, height:, :] = jnp.zeros((2, Z * Y, full - height, width), held.dtype)
        steps = rows - 1 + core * (2 - rows), 1 + core * (rows - 2)
        for ref, step in (own_ref, 0), (near_ref, steps[0]), (other_ref, steps[1]), (far_ref, 2):
            block_row = lax.rem(x + step, rows)
            half = block_row // (rows // 2)
            for i in range(count):
                there = lax.rem(block_row, rows // 2) * count + i
                dz = lax.rem(there // Y - z + Z, Z)
                dy = lax.rem(i % Y - y + Y, Y)
                oz = jnp.where(dz < Z // 2, 2 * dz, 2 * (Z - dz) - 1)
                oy = jnp.where(dy < Y // 2, 2 * dy, 2 * (Y - dy) - 1)
                place = jnp.where(half == 0, oz * Y + oy, oz // Y * (Y * Y) + oy * Y + lax.rem(oz, Y))
                held[lax.rem(half + core, 2), place, pl.ds(0, height), :] = ref[pl.ds(i * height, height), :]
        at = [0, 0]
        for out_ref, (side, blocks) in zip(out_refs, cuts):
            part = held[side, pl.ds(at[side], blocks)].reshape(blocks * full, width)
            out_ref[...] = part if out_ref is out_refs[-1] else part.T
            at[side] += blocks

    size = 2 * own.size * rows
    shapes = [(width, blocks * full) for _, blocks in cuts]
    shapes[-1] = shapes[-1][::-1]
    factors = pl.pallas_call(
        kernel,
        out_shape=[jax.ShapeDtypeStruct(shape, own.dtype) for shape in shapes],
        scratch_shapes=[pltpu.VMEM((2, Z * Y, full, width), own.dtype)],
        compiler_params=pltpu.CompilerParams(vmem_limit_bytes=VMEM),
        cost_estimate=pl.CostEstimate(flops=0, bytes_accessed=2 * size, transcendentals=0),
        name="arrange",
    )(own, near, other, far)
    return factors[:3], factors[3:]


def products(refs, counts, start, width):
    share, at = 0.0, 0
    for count in counts:
        part = jnp.concatenate([ref[:, pl.ds(start, width)] for ref in refs[at + 1 : at + 1 + count]])
        share += jnp.dot(refs[at][...], part, preferred_element_type=jnp.float32)
        at += count + 1
    return share


def multiply(body, shape, factors, pieces, *operands, **options):
    columns = pieces[0][0].shape[-1]
    flops = 2 * sum(factor.size for factor in factors) * columns
    flat = []
    for factor, group in zip(factors, pieces):
        flat += [factor, *[piece.reshape(-1, columns) for piece in group]]
    return pl.pallas_call(
        body,
        out_shape=jax.ShapeDtypeStruct(shape, jnp.float32),
        compiler_params=pltpu.CompilerParams(vmem_limit_bytes=VMEM),
        cost_estimate=pl.CostEstimate(flops=flops, bytes_accessed=flops // 512, transcendentals=0),
        **options,
    )(*operands, *flat)


def tiles(columns, tile=256):
    return [(start, min(tile, columns - start)) for start in range(0, columns, tile)]


def first_products(factors, pieces):
    counts = [len(group) for group in pieces]

    def body(*refs):
        for start, width in tiles(refs[-1].shape[1]):
            refs[-1][:, pl.ds(start, width)] = products(refs, counts, start, width)

    return multiply(body, (factors[0].shape[0], pieces[0][0].shape[-1]), factors, pieces, name="first")


def second_products(total, factors, pieces):
    counts = [len(group) for group in pieces]

    def body(total_ref, *refs):
        for start, width in tiles(refs[-1].shape[1]):
            part = pl.ds(start, width)
            refs[-1][:, part] = total_ref[:, part] + products(refs, counts, start, width)

    return multiply(body, total.shape, factors, pieces, total, name="second")


def more_products(residual, total, factors, pieces):
    counts = [len(group) for group in pieces]

    def body(residual_ref, total_ref, *refs):
        for start, width in tiles(refs[-1].shape[0]):
            part = pl.ds(start, width)
            share = total_ref[:, part] + products(refs, counts, start, width)
            refs[-1][part, :] = residual_ref[part, :] + share.T

    return multiply(body, residual.shape, factors, pieces, residual, total, name="more")


def last_products(total, factor, pieces):
    parts = tiles(total.shape[0])

    def body(total_ref, factor_ref, *refs):
        *piece_refs, out_ref, held, sems = refs
        copies = []
        for number, (start, width) in enumerate(parts):
            part = pl.ds(start, width)
            piece = jnp.concatenate([ref[:, part] for ref in piece_refs])
            share = lax.dot_general(piece, factor_ref[...], (((0,), (0,)), ((), ())), preferred_element_type=jnp.float32)
            held[part, :] = total_ref[part, :] + share
            copies.append(pltpu.make_async_copy(held.at[part], out_ref.at[part], sems.at[number]))
            copies[-1].start()
        for copy in copies:
            copy.wait()

    return multiply(
        body,
        total.shape,
        [factor],
        [pieces],
        total,
        out_specs=pl.BlockSpec(memory_space=pl.ANY),
        scratch_shapes=[pltpu.VMEM(total.shape, jnp.float32), pltpu.SemaphoreType.DMA((len(parts),))],
        name="last",
    )


def solution(mesh):
    rows = mesh.shape["row"]

    def per_device(residual_in, integrals, amplitudes):
        height = integrals.shape[1]
        block = padded(integrals.T, height)
        return ladder(block, height, amplitudes, rows, residual_in.T).T

    placed = (P(("col", "depth"), "row"), P("row", ("col", "depth")), P("row", ("col", "depth")))
    return jax.shard_map(
        per_device, mesh=mesh, in_specs=placed, out_specs=P(("col", "depth"), "row"), check_vma=False
    )
```

```python
import jax
import jax.numpy as jnp
from jax import lax
from jax.experimental import pallas as pl
from jax.experimental.pallas import tpu as pltpu
from jax.sharding import PartitionSpec as P

Z, Y = 8, 4
VMEM = 16 << 20


def along_row(array, size, first, second):
    pairs = [((row * 2 + core), (row + step) % size * 2 + core) for row in range(size) for core, step in enumerate((first, second))]
    return lax.ppermute(array, ("row", "col"), pairs)


def travel(array, first, second):
    pairs = []
    for core, step in enumerate((first, second)):
        if step is not None:
            for z in range(Z):
                for y in range(Y):
                    target = (z + step[0]) % Z * Y + (y + step[1]) % Y
                    pairs.append(((core * Z + z) * Y + y, core * Z * Y + target))
    return lax.ppermute(array, ("col", "depth"), pairs)


def swap(array):
    return lax.ppermute(array, "col", [(0, 1), (1, 0)])


def packed(*blocks):
    return jnp.concatenate([jnp.pad(block, ((0, 0), (0, -block.shape[1] % 8), (0, 0))) for block in blocks])


def ladder(block, height, amplitudes, rows, residual):
    along, back = ((0, 1), (1, 0)), ((0, -1), (-1, 0))
    up, down = ((1, 0), (0, 1)), ((-1, 0), (0, -1))
    near = along_row(amplitudes, rows, 1, -1)
    a1 = travel(block, *along)
    b1 = travel(block, *back)
    a2 = travel(a1, *along)
    pack = packed(block, a1, b1, a2)
    b2 = travel(b1, None, back[1])
    a3 = travel(a2, None, along[1])
    own, near, b2, a3 = lax.optimization_barrier((amplitudes, near, b2, a3))
    other = along_row(own, rows, -1, 1)
    b3 = travel(b2, None, back[1])
    a4 = travel(a3, None, along[1])
    near_again, b3 = lax.optimization_barrier((near, b3))
    far = along_row(near_again, rows, 1, -1)
    rest = lax.optimization_barrier(packed(b2, a3, b3, a4))
    u1, d1 = travel(pack, *up), travel(pack, *down)
    u2, d2 = travel(u1, *up), travel(d1, down[0], None)
    u2, d2, other = lax.optimization_barrier((u2, d2, other))
    first = lax.axis_index("col") == 0
    kept = jnp.where(first, d2, rest)
    u3, d3 = travel(jnp.where(first, u2, rest), *up), travel(kept, *down)
    theirs = [swap(piece) for piece in (pack, u1, d1, u2, kept)]
    own_factors, their_factors = arrange(amplitudes, near, other, far, rows, height)
    total = first_products([own_factors[0], their_factors[0]], [[pack, u1], theirs[:2]])
    u3, d3, total = lax.optimization_barrier((u3, d3, total))
    u4, d4 = travel(u3[:2], *up), travel(d3[2:], *down)
    total = second_products(total, [own_factors[1], their_factors[1]], [[d1, u2, kept], theirs[2:]])
    theirs = [swap(u3), swap(d3)]
    u4, d4, total = lax.optimization_barrier((u4, d4, total))
    total = more_products(residual, total, [own_factors[2], their_factors[2]], [[u3, d3, u4, d4], theirs])
    return last_products(total, their_factors[3], [swap(u4), swap(d4)])


def arrange(own, near, other, far, rows, height):
    cuts = [(0, blocks) for blocks in (8, 12, 12)] + [(1, blocks) for blocks in (8, 12, 8, 4)]
    width = own.shape[1]
    count = own.shape[0] // height
    full = height + -height % 8

    def kernel(own_ref, near_ref, other_ref, far_ref, *refs):
        out_refs, held = refs[:-1], refs[-1]
        x, core, depth = (lax.axis_index(name) for name in ("row", "col", "depth"))
        z, y = depth // Y, lax.rem(depth, Y)
        held[:, :, height:, :] = jnp.zeros((2, Z * Y, full - height, width), held.dtype)
        steps = rows - 1 + core * (2 - rows), 1 + core * (rows - 2)
        for ref, step in (own_ref, 0), (near_ref, steps[0]), (other_ref, steps[1]), (far_ref, 2):
            block_row = lax.rem(x + step, rows)
            half = block_row // (rows // 2)
            for i in range(count):
                there = lax.rem(block_row, rows // 2) * count + i
                dz = lax.rem(there // Y - z + Z, Z)
                dy = lax.rem(i % Y - y + Y, Y)
                oz = jnp.where(dz < Z // 2, 2 * dz, 2 * (Z - dz) - 1)
                oy = jnp.where(dy < Y // 2, 2 * dy, 2 * (Y - dy) - 1)
                place = jnp.where(half == 0, oz * Y + oy, oz // Y * (Y * Y) + oy * Y + lax.rem(oz, Y))
                held[lax.rem(half + core, 2), place, pl.ds(0, height), :] = ref[pl.ds(i * height, height), :]
        at = [0, 0]
        for out_ref, (side, blocks) in zip(out_refs, cuts):
            part = held[side, pl.ds(at[side], blocks)].reshape(blocks * full, width)
            out_ref[...] = part if out_ref is out_refs[-1] else part.T
            at[side] += blocks

    size = 2 * own.size * rows
    shapes = [(width, blocks * full) for _, blocks in cuts]
    shapes[-1] = shapes[-1][::-1]
    factors = pl.pallas_call(
        kernel,
        out_shape=[jax.ShapeDtypeStruct(shape, own.dtype) for shape in shapes],
        scratch_shapes=[pltpu.VMEM((2, Z * Y, full, width), own.dtype)],
        compiler_params=pltpu.CompilerParams(vmem_limit_bytes=VMEM),
        cost_estimate=pl.CostEstimate(flops=0, bytes_accessed=2 * size, transcendentals=0),
        name="arrange",
    )(own, near, other, far)
    return factors[:3], factors[3:]


def products(refs, counts, start, width):
    share, at = 0.0, 0
    for count in counts:
        part = jnp.concatenate([ref[:, pl.ds(start, width)] for ref in refs[at + 1 : at + 1 + count]])
        share += jnp.dot(refs[at][...], part, preferred_element_type=jnp.float32)
        at += count + 1
    return share


def multiply(body, shape, factors, pieces, *operands, **options):
    columns = pieces[0][0].shape[-1]
    flops = 2 * sum(factor.size for factor in factors) * columns
    flat = []
    for factor, group in zip(factors, pieces):
        flat += [factor, *[piece.reshape(-1, columns) for piece in group]]
    return pl.pallas_call(
        body,
        out_shape=jax.ShapeDtypeStruct(shape, jnp.float32),
        compiler_params=pltpu.CompilerParams(vmem_limit_bytes=VMEM),
        cost_estimate=pl.CostEstimate(flops=flops, bytes_accessed=flops // 512, transcendentals=0),
        **options,
    )(*operands, *flat)


def tiles(columns, tile=256):
    return [(start, min(tile, columns - start)) for start in range(0, columns, tile)]


def first_products(factors, pieces):
    counts = [len(group) for group in pieces]

    def body(*refs):
        for start, width in tiles(refs[-1].shape[1]):
            refs[-1][:, pl.ds(start, width)] = products(refs, counts, start, width)

    return multiply(body, (factors[0].shape[0], pieces[0][0].shape[-1]), factors, pieces, name="first")


def second_products(total, factors, pieces):
    counts = [len(group) for group in pieces]

    def body(total_ref, *refs):
        for start, width in tiles(refs[-1].shape[1]):
            part = pl.ds(start, width)
            refs[-1][:, part] = total_ref[:, part] + products(refs, counts, start, width)

    return multiply(body, total.shape, factors, pieces, total, name="second")


def more_products(residual, total, factors, pieces):
    counts = [len(group) for group in pieces]

    def body(residual_ref, total_ref, *refs):
        for start, width in tiles(refs[-1].shape[0]):
            part = pl.ds(start, width)
            share = total_ref[:, part] + products(refs, counts, start, width)
            refs[-1][part, :] = residual_ref[part, :] + share.T

    return multiply(body, residual.shape, factors, pieces, residual, total, name="more")


def last_products(total, factor, pieces):
    parts = tiles(total.shape[0])

    def body(total_ref, factor_ref, *refs):
        *piece_refs, out_ref, held, sems = refs
        copies = []
        for number, (start, width) in enumerate(parts):
            part = pl.ds(start, width)
            piece = jnp.concatenate([ref[:, part] for ref in piece_refs])
            share = lax.dot_general(piece, factor_ref[...], (((0,), (0,)), ((), ())), preferred_element_type=jnp.float32)
            held[part, :] = total_ref[part, :] + share
            copies.append(pltpu.make_async_copy(held.at[part], out_ref.at[part], sems.at[number]))
            copies[-1].start()
        for copy in copies:
            copy.wait()

    return multiply(
        body,
        total.shape,
        [factor],
        [pieces],
        total,
        out_specs=pl.BlockSpec(memory_space=pl.ANY),
        scratch_shapes=[pltpu.VMEM(total.shape, jnp.float32), pltpu.SemaphoreType.DMA((len(parts),))],
        name="last",
    )


def solution(mesh):
    rows = mesh.shape["row"]

    def per_device(residual_in, integrals, amplitudes):
        height = integrals.shape[1]
        return ladder(integrals.T[None], height, amplitudes, rows, residual_in.T).T

    placed = (P(("col", "depth"), "row"), P("row", ("col", "depth")), P("row", ("col", "depth")))
    return jax.shard_map(
        per_device, mesh=mesh, in_specs=placed, out_specs=P(("col", "depth"), "row"), check_vma=False
    )
```

```python
import jax
import jax.numpy as jnp
from jax import lax
from jax.experimental import pallas as pl
from jax.experimental.pallas import tpu as pltpu
from jax.sharding import PartitionSpec as P

Z, Y = 8, 4
VMEM = 16 << 20


def along_row(array, size, first, second):
    pairs = [((row * 2 + core), (row + step) % size * 2 + core) for row in range(size) for core, step in enumerate((first, second))]
    return lax.ppermute(array, ("row", "col"), pairs)


def travel(array, first, second):
    pairs = []
    for core, step in enumerate((first, second)):
        if step is not None:
            for z in range(Z):
                for y in range(Y):
                    target = (z + step[0]) % Z * Y + (y + step[1]) % Y
                    pairs.append(((core * Z + z) * Y + y, core * Z * Y + target))
    return lax.ppermute(array, ("col", "depth"), pairs)


def swap(array):
    return lax.ppermute(array, "col", [(0, 1), (1, 0)])


def packed(*blocks):
    return jnp.concatenate([jnp.pad(block, ((0, 0), (0, -block.shape[1] % 8), (0, 0))) for block in blocks])


def ladder(block, height, amplitudes, rows, residual):
    along, back = ((0, 1), (1, 0)), ((0, -1), (-1, 0))
    up, down = ((1, 0), (0, 1)), ((-1, 0), (0, -1))
    near = along_row(amplitudes, rows, 1, -1)
    a1 = travel(block, *along)
    b1 = travel(block, *back)
    a2 = travel(a1, *along)
    pack = packed(block, a1, b1, a2)
    b2 = travel(b1, None, back[1])
    a3 = travel(a2, None, along[1])
    own, near, b2, a3 = lax.optimization_barrier((amplitudes, near, b2, a3))
    other = along_row(own, rows, -1, 1)
    b3 = travel(b2, None, back[1])
    a4 = travel(a3, None, along[1])
    near_again, b3 = lax.optimization_barrier((near, b3))
    far = along_row(near_again, rows, 1, -1)
    rest = lax.optimization_barrier(packed(b2, a3, b3, a4))
    u1, d1 = travel(pack, *up), travel(pack, *down)
    u2, d2 = travel(u1, *up), travel(d1, down[0], None)
    u2, d2, other = lax.optimization_barrier((u2, d2, other))
    first = lax.axis_index("col") == 0
    kept = jnp.where(first, d2, rest)
    u3, d3 = travel(jnp.where(first, u2, rest), *up), travel(kept, *down)
    theirs = [swap(piece) for piece in (pack, u1, d1, u2, kept)]
    own_factors, their_factors = arrange(amplitudes, near, other, far, rows, height)
    theirs[:2] = lax.optimization_barrier(theirs[:2])
    total = first_products([own_factors[0], their_factors[0]], [[pack], theirs[:1]])
    u3, d3, total = lax.optimization_barrier((u3, d3, total))
    u4, d4 = travel(u3[:2], *up), travel(d3[2:], *down)
    total = second_products(total, [own_factors[1], their_factors[1]], [[u1, d1, u2, kept], theirs[1:]])
    theirs = [swap(u3), swap(d3)]
    u4, d4, total = lax.optimization_barrier((u4, d4, total))
    total = more_products(residual, total, [own_factors[2], their_factors[2]], [[u3, d3, u4, d4], theirs])
    return last_products(total, their_factors[3], [swap(u4), swap(d4)])


def arrange(own, near, other, far, rows, height):
    cuts = [(0, blocks) for blocks in (4, 16, 12)] + [(1, blocks) for blocks in (4, 16, 8, 4)]
    width = own.shape[1]
    count = own.shape[0] // height
    full = height + -height % 8

    def kernel(own_ref, near_ref, other_ref, far_ref, *refs):
        out_refs, held = refs[:-1], refs[-1]
        x, core, depth = (lax.axis_index(name) for name in ("row", "col", "depth"))
        z, y = depth // Y, lax.rem(depth, Y)
        held[:, :, height:, :] = jnp.zeros((2, Z * Y, full - height, width), held.dtype)
        steps = rows - 1 + core * (2 - rows), 1 + core * (rows - 2)
        for ref, step in (own_ref, 0), (near_ref, steps[0]), (other_ref, steps[1]), (far_ref, 2):
            block_row = lax.rem(x + step, rows)
            half = block_row // (rows // 2)
            for i in range(count):
                there = lax.rem(block_row, rows // 2) * count + i
                dz = lax.rem(there // Y - z + Z, Z)
                dy = lax.rem(i % Y - y + Y, Y)
                oz = jnp.where(dz < Z // 2, 2 * dz, 2 * (Z - dz) - 1)
                oy = jnp.where(dy < Y // 2, 2 * dy, 2 * (Y - dy) - 1)
                place = jnp.where(half == 0, oz * Y + oy, oz // Y * (Y * Y) + oy * Y + lax.rem(oz, Y))
                held[lax.rem(half + core, 2), place, pl.ds(0, height), :] = ref[pl.ds(i * height, height), :]
        at = [0, 0]
        for out_ref, (side, blocks) in zip(out_refs, cuts):
            part = held[side, pl.ds(at[side], blocks)].reshape(blocks * full, width)
            out_ref[...] = part if out_ref is out_refs[-1] else part.T
            at[side] += blocks

    size = 2 * own.size * rows
    shapes = [(width, blocks * full) for _, blocks in cuts]
    shapes[-1] = shapes[-1][::-1]
    factors = pl.pallas_call(
        kernel,
        out_shape=[jax.ShapeDtypeStruct(shape, own.dtype) for shape in shapes],
        scratch_shapes=[pltpu.VMEM((2, Z * Y, full, width), own.dtype)],
        compiler_params=pltpu.CompilerParams(vmem_limit_bytes=VMEM),
        cost_estimate=pl.CostEstimate(flops=0, bytes_accessed=2 * size, transcendentals=0),
        name="arrange",
    )(own, near, other, far)
    return factors[:3], factors[3:]


def products(refs, counts, start, width):
    share, at = 0.0, 0
    for count in counts:
        part = jnp.concatenate([ref[:, pl.ds(start, width)] for ref in refs[at + 1 : at + 1 + count]])
        share += jnp.dot(refs[at][...], part, preferred_element_type=jnp.float32)
        at += count + 1
    return share


def multiply(body, shape, factors, pieces, *operands, **options):
    columns = pieces[0][0].shape[-1]
    flops = 2 * sum(factor.size for factor in factors) * columns
    flat = []
    for factor, group in zip(factors, pieces):
        flat += [factor, *[piece.reshape(-1, columns) for piece in group]]
    return pl.pallas_call(
        body,
        out_shape=jax.ShapeDtypeStruct(shape, jnp.float32),
        compiler_params=pltpu.CompilerParams(vmem_limit_bytes=VMEM),
        cost_estimate=pl.CostEstimate(flops=flops, bytes_accessed=flops // 512, transcendentals=0),
        **options,
    )(*operands, *flat)


def tiles(columns, tile=256):
    return [(start, min(tile, columns - start)) for start in range(0, columns, tile)]


def first_products(factors, pieces):
    counts = [len(group) for group in pieces]

    def body(*refs):
        for start, width in tiles(refs[-1].shape[1]):
            refs[-1][:, pl.ds(start, width)] = products(refs, counts, start, width)

    return multiply(body, (factors[0].shape[0], pieces[0][0].shape[-1]), factors, pieces, name="first")


def second_products(total, factors, pieces):
    counts = [len(group) for group in pieces]

    def body(total_ref, *refs):
        for start, width in tiles(refs[-1].shape[1]):
            part = pl.ds(start, width)
            refs[-1][:, part] = total_ref[:, part] + products(refs, counts, start, width)

    return multiply(body, total.shape, factors, pieces, total, name="second")


def more_products(residual, total, factors, pieces):
    counts = [len(group) for group in pieces]

    def body(residual_ref, total_ref, *refs):
        for start, width in tiles(refs[-1].shape[0]):
            part = pl.ds(start, width)
            share = total_ref[:, part] + products(refs, counts, start, width)
            refs[-1][part, :] = residual_ref[part, :] + share.T

    return multiply(body, residual.shape, factors, pieces, residual, total, name="more")


def last_products(total, factor, pieces):
    parts = tiles(total.shape[0])

    def body(total_ref, factor_ref, *refs):
        *piece_refs, out_ref, held, sems = refs
        copies = []
        for number, (start, width) in enumerate(parts):
            part = pl.ds(start, width)
            piece = jnp.concatenate([ref[:, part] for ref in piece_refs])
            share = lax.dot_general(piece, factor_ref[...], (((0,), (0,)), ((), ())), preferred_element_type=jnp.float32)
            held[part, :] = total_ref[part, :] + share
            copies.append(pltpu.make_async_copy(held.at[part], out_ref.at[part], sems.at[number]))
            copies[-1].start()
        for copy in copies:
            copy.wait()

    return multiply(
        body,
        total.shape,
        [factor],
        [pieces],
        total,
        out_specs=pl.BlockSpec(memory_space=pl.ANY),
        scratch_shapes=[pltpu.VMEM(total.shape, jnp.float32), pltpu.SemaphoreType.DMA((len(parts),))],
        name="last",
    )


def solution(mesh):
    rows = mesh.shape["row"]

    def per_device(residual_in, integrals, amplitudes):
        height = integrals.shape[1]
        return ladder(integrals.T[None], height, amplitudes, rows, residual_in.T).T

    placed = (P(("col", "depth"), "row"), P("row", ("col", "depth")), P("row", ("col", "depth")))
    return jax.shard_map(
        per_device, mesh=mesh, in_specs=placed, out_specs=P(("col", "depth"), "row"), check_vma=False
    )
```

```python
import jax
import jax.numpy as jnp
from jax import lax
from jax.experimental import pallas as pl
from jax.experimental.pallas import tpu as pltpu
from jax.sharding import PartitionSpec as P

Z, Y = 8, 4
VMEM = 16 << 20


def along_row(array, size, first, second):
    pairs = [((row * 2 + core), (row + step) % size * 2 + core) for row in range(size) for core, step in enumerate((first, second))]
    return lax.ppermute(array, ("row", "col"), pairs)


def travel(array, first, second):
    pairs = []
    for core, step in enumerate((first, second)):
        if step is not None:
            for z in range(Z):
                for y in range(Y):
                    target = (z + step[0]) % Z * Y + (y + step[1]) % Y
                    pairs.append(((core * Z + z) * Y + y, core * Z * Y + target))
    return lax.ppermute(array, ("col", "depth"), pairs)


def swap(array):
    return lax.ppermute(array, "col", [(0, 1), (1, 0)])


def packed(*blocks):
    return jnp.concatenate([jnp.pad(block, ((0, 0), (0, -block.shape[1] % 8), (0, 0))) for block in blocks])


def ladder(block, height, amplitudes, rows, residual):
    along, back = ((0, 1), (1, 0)), ((0, -1), (-1, 0))
    up, down = ((1, 0), (0, 1)), ((-1, 0), (0, -1))
    near = along_row(amplitudes, rows, 1, -1)
    a1 = travel(block, *along)
    b1 = travel(block, *back)
    a2 = travel(a1, *along)
    pack = packed(block, a1, b1, a2)
    b2 = travel(b1, None, back[1])
    a3 = travel(a2, None, along[1])
    own, near, b2, a3 = lax.optimization_barrier((amplitudes, near, b2, a3))
    other = along_row(own, rows, -1, 1)
    b3 = travel(b2, None, back[1])
    a4 = travel(a3, None, along[1])
    near_again, b3 = lax.optimization_barrier((near, b3))
    far = along_row(near_again, rows, 1, -1)
    rest = lax.optimization_barrier(packed(b2, a3, b3, a4))
    u1, d1 = travel(pack, *up), travel(pack, *down)
    u2, d2 = travel(u1, *up), travel(d1, down[0], None)
    u2, d2, other = lax.optimization_barrier((u2, d2, other))
    first = lax.axis_index("col") == 0
    kept = jnp.where(first, d2, rest)
    u3, d3 = travel(jnp.where(first, u2, rest), *up), travel(kept, *down)
    theirs = [swap(piece) for piece in (pack, u1, d1, u2, kept)]
    own_factors, their_factors = arrange(amplitudes, near, other, far, rows, height)
    theirs[:2] = lax.optimization_barrier(theirs[:2])
    total = first_products([own_factors[0], their_factors[0]], [[pack], theirs[:1]])
    u3, d3, total = lax.optimization_barrier((u3, d3, total))
    halves = [u3[:2], u3[2:]]
    u4, d4 = travel(halves[0], *up), travel(d3[2:], *down)
    total = second_products(total, [own_factors[1], their_factors[1]], [[u1, d1, u2, kept], theirs[1:]])
    theirs = [*[swap(piece) for piece in halves], swap(d3)]
    u4, d4, total = lax.optimization_barrier((u4, d4, total))
    total = more_products(residual, total, [own_factors[2], their_factors[2]], [[u3, d3, u4, d4], theirs])
    return last_products(total, their_factors[3], [swap(u4), swap(d4)])


def arrange(own, near, other, far, rows, height):
    cuts = [(0, blocks) for blocks in (4, 16, 12)] + [(1, blocks) for blocks in (4, 16, 8, 4)]
    width = own.shape[1]
    count = own.shape[0] // height
    full = height + -height % 8

    def kernel(own_ref, near_ref, other_ref, far_ref, *refs):
        out_refs, held = refs[:-1], refs[-1]
        x, core, depth = (lax.axis_index(name) for name in ("row", "col", "depth"))
        z, y = depth // Y, lax.rem(depth, Y)
        held[:, :, height:, :] = jnp.zeros((2, Z * Y, full - height, width), held.dtype)
        steps = rows - 1 + core * (2 - rows), 1 + core * (rows - 2)
        for ref, step in (own_ref, 0), (near_ref, steps[0]), (other_ref, steps[1]), (far_ref, 2):
            block_row = lax.rem(x + step, rows)
            half = block_row // (rows // 2)
            for i in range(count):
                there = lax.rem(block_row, rows // 2) * count + i
                dz = lax.rem(there // Y - z + Z, Z)
                dy = lax.rem(i % Y - y + Y, Y)
                oz = jnp.where(dz < Z // 2, 2 * dz, 2 * (Z - dz) - 1)
                oy = jnp.where(dy < Y // 2, 2 * dy, 2 * (Y - dy) - 1)
                place = jnp.where(half == 0, oz * Y + oy, oz // Y * (Y * Y) + oy * Y + lax.rem(oz, Y))
                held[lax.rem(half + core, 2), place, pl.ds(0, height), :] = ref[pl.ds(i * height, height), :]
        at = [0, 0]
        for out_ref, (side, blocks) in zip(out_refs, cuts):
            part = held[side, pl.ds(at[side], blocks)].reshape(blocks * full, width)
            out_ref[...] = part if out_ref is out_refs[-1] else part.T
            at[side] += blocks

    size = 2 * own.size * rows
    shapes = [(width, blocks * full) for _, blocks in cuts]
    shapes[-1] = shapes[-1][::-1]
    factors = pl.pallas_call(
        kernel,
        out_shape=[jax.ShapeDtypeStruct(shape, own.dtype) for shape in shapes],
        scratch_shapes=[pltpu.VMEM((2, Z * Y, full, width), own.dtype)],
        compiler_params=pltpu.CompilerParams(vmem_limit_bytes=VMEM),
        cost_estimate=pl.CostEstimate(flops=0, bytes_accessed=2 * size, transcendentals=0),
        name="arrange",
    )(own, near, other, far)
    return factors[:3], factors[3:]


def products(refs, counts, start, width):
    share, at = 0.0, 0
    for count in counts:
        part = jnp.concatenate([ref[:, pl.ds(start, width)] for ref in refs[at + 1 : at + 1 + count]])
        share += jnp.dot(refs[at][...], part, preferred_element_type=jnp.float32)
        at += count + 1
    return share


def multiply(body, shape, factors, pieces, *operands, **options):
    columns = pieces[0][0].shape[-1]
    flops = 2 * sum(factor.size for factor in factors) * columns
    flat = []
    for factor, group in zip(factors, pieces):
        flat += [factor, *[piece.reshape(-1, columns) for piece in group]]
    return pl.pallas_call(
        body,
        out_shape=jax.ShapeDtypeStruct(shape, jnp.float32),
        compiler_params=pltpu.CompilerParams(vmem_limit_bytes=VMEM),
        cost_estimate=pl.CostEstimate(flops=flops, bytes_accessed=flops // 512, transcendentals=0),
        **options,
    )(*operands, *flat)


def tiles(columns, tile=256):
    return [(start, min(tile, columns - start)) for start in range(0, columns, tile)]


def first_products(factors, pieces):
    counts = [len(group) for group in pieces]

    def body(*refs):
        for start, width in tiles(refs[-1].shape[1]):
            refs[-1][:, pl.ds(start, width)] = products(refs, counts, start, width)

    return multiply(body, (factors[0].shape[0], pieces[0][0].shape[-1]), factors, pieces, name="first")


def second_products(total, factors, pieces):
    counts = [len(group) for group in pieces]

    def body(total_ref, *refs):
        for start, width in tiles(refs[-1].shape[1]):
            part = pl.ds(start, width)
            refs[-1][:, part] = total_ref[:, part] + products(refs, counts, start, width)

    return multiply(body, total.shape, factors, pieces, total, name="second")


def more_products(residual, total, factors, pieces):
    counts = [len(group) for group in pieces]

    def body(residual_ref, total_ref, *refs):
        for start, width in tiles(refs[-1].shape[0]):
            part = pl.ds(start, width)
            share = total_ref[:, part] + products(refs, counts, start, width)
            refs[-1][part, :] = residual_ref[part, :] + share.T

    return multiply(body, residual.shape, factors, pieces, residual, total, name="more")


def last_products(total, factor, pieces):
    parts = tiles(total.shape[0])

    def body(total_ref, factor_ref, *refs):
        *piece_refs, out_ref, held, sems = refs
        copies = []
        for number, (start, width) in enumerate(parts):
            part = pl.ds(start, width)
            piece = jnp.concatenate([ref[:, part] for ref in piece_refs])
            share = lax.dot_general(piece, factor_ref[...], (((0,), (0,)), ((), ())), preferred_element_type=jnp.float32)
            held[part, :] = total_ref[part, :] + share
            copies.append(pltpu.make_async_copy(held.at[part], out_ref.at[part], sems.at[number]))
            copies[-1].start()
        for copy in copies:
            copy.wait()

    return multiply(
        body,
        total.shape,
        [factor],
        [pieces],
        total,
        out_specs=pl.BlockSpec(memory_space=pl.ANY),
        scratch_shapes=[pltpu.VMEM(total.shape, jnp.float32), pltpu.SemaphoreType.DMA((len(parts),))],
        name="last",
    )


def solution(mesh):
    rows = mesh.shape["row"]

    def per_device(residual_in, integrals, amplitudes):
        height = integrals.shape[1]
        return ladder(integrals.T[None], height, amplitudes, rows, residual_in.T).T

    placed = (P(("col", "depth"), "row"), P("row", ("col", "depth")), P("row", ("col", "depth")))
    return jax.shard_map(
        per_device, mesh=mesh, in_specs=placed, out_specs=P(("col", "depth"), "row"), check_vma=False
    )
```
